256 devices in a mesh: ctx: 32 (over y, x, core), tp: 8 (over z).
Axes of the slice: x: 4, y: 4, z: 8, core: 2. Of those that a mesh axis runs over, the one named last changes fastest.
Arguments:
- queries: bfloat16 [8192, 4096], P('ctx', 'tp'), may hold values from -120 to 120
- keys: bfloat16 [8192, 4096], P('ctx', 'tp'), may hold values from -7 to 7
- values: bfloat16 [8192, 4096], P('ctx', 'tp'), may hold values from -7 to 7
- out_weight: bfloat16 [4096, 4096], P(None, 'tp'), may hold values from -0.09375 to 0.09375
- out_grad: bfloat16 [8192, 4096], P('ctx', 'tp'), may hold values from -48 to 48
Outputs:
- mixed: bfloat16 [8192, 4096], P('ctx', 'tp')
- grad_queries: bfloat16 [8192, 4096], P('ctx', 'tp')
- grad_keys: bfloat16 [8192, 4096], P('ctx', 'tp')
- grad_values: bfloat16 [8192, 4096], P('ctx', 'tp')
- grad_weight: float32 [4096, 4096], P('ctx', 'tp')
The draws below stay inside these ranges and needn't reach their ends.
All inputs are finite; a program needn't handle non-finite values.
Results may differ from the reference program's by a relative error of at most 0.02.
Values may be sent and summed in bfloat16 or wider, within the bound.
No kernel may reach another device: no remote copies, remote signals or barrier semaphores. Data moves between devices by JAX's collectives and lax.ppermute only.
A program may use at most 128 MiB of HBM per device.

```python
import math
import jax
import jax.numpy as jnp
from jax import lax

D = 4096
HEADS = 32
HEAD_DIM = 128
BLOCK = 16
HD = 4096
TOKENS = 8192
HEAD_GROUPS = 8
LEVELS = 9


def multiscale(key, white):
    count_rows = TOKENS
    total = white * jax.random.normal(key, (count_rows, HD), jnp.float32)
    spans = list(range(2, count_rows.bit_length() - 1, 2))
    weight = math.sqrt((1.0 - white * white) / len(spans))
    for span in spans:
        coarse = jax.random.normal(jax.random.fold_in(key, 50 + span), (count_rows >> span, HD), jnp.float32)
        total = total + weight * jnp.repeat(coarse, 2 ** span, axis=0)
    return jnp.clip(total, -7.0, 7.0)


def key_field(key):
    base = multiscale(jax.random.fold_in(key, 11), 0.6)
    order = jnp.arange(TOKENS)[:, None] % 256
    return jnp.where(order == 3, base, base)


def draw_keys(key, part):
    field = key_field(key)
    return field.astype(jnp.bfloat16)


def draw_queries(key, part):
    key = jax.random.fold_in(key, 3)
    noise = jax.random.normal(key, (TOKENS, HD), jnp.float32)
    return jnp.clip(noise, -120.0, 120.0).astype(jnp.bfloat16)


def draw_values(key, part):
    key = jax.random.fold_in(key, 7)
    field = multiscale(key, 0.6)
    return jnp.clip(field, -7.0, 7.0).astype(jnp.bfloat16)


def spiked(values, stream_key, source, target, blocks, factor):
    def block_of(axis_at):
        return (jnp.arange(values.shape[axis_at]) // (values.shape[axis_at] // blocks)).reshape((-1,) + (1,) * (values.ndim - 1 - axis_at))

    one_side = jax.random.permutation(stream_key, blocks)[block_of(target)]
    second = (block_of(target) + blocks // 2) % blocks
    return jnp.where((block_of(source) == one_side) | (block_of(source) == second), factor * values, values)


def block_levels(key, shape, cuts, least, largest):
    def one(dim, blocks):
        steps = jax.random.uniform(jax.random.fold_in(jax.random.fold_in(key, 6), dim), (blocks,), jnp.float32, least / len(cuts), largest / len(cuts))
        return jnp.repeat(jnp.exp(steps), shape[dim] // blocks).reshape((-1,) + (1,) * (len(shape) - dim - 1))

    level = one(*cuts[0])
    for cut in cuts[1:]:
        level = level * one(*cut)
    return level


def centred(rng, extent, width, limit, shards=(), dtype=jnp.bfloat16):
    factor_of = block_levels(rng, extent, shards, -0.22, 0.18) if shards else 1.0
    entries = jax.random.normal(rng, extent, jnp.float32) * width * factor_of
    return jnp.minimum(jnp.maximum(entries, -limit), limit).astype(dtype)


def heavy_noise(stream_key, shape, deviation, limit, cuts, heavy, held_as=jnp.bfloat16):
    values = deviation * jax.random.normal(stream_key, shape, jnp.float32)
    if cuts:
        values = values * block_levels(stream_key, shape, cuts, -0.22, 0.18)
    return jnp.clip(spiked(values, jax.random.fold_in(stream_key, 3), *heavy), -limit, limit).astype(held_as)


def setup_inputs(seed: int = 0) -> dict:
    splits = jax.random.split(jax.random.key(seed), 6)
    queries = draw_queries(jax.random.fold_in(splits[5], 71), 0)
    keys = draw_keys(jax.random.fold_in(splits[5], 71), 0)
    values = draw_values(jax.random.fold_in(splits[5], 71), 0)
    out_weight = centred(splits[3], (D, HD), HD ** -0.5, 0.09375, ((1, 8),))
    out_grad = heavy_noise(splits[4], (TOKENS, D), 4.0, 48.0, ((0, 32), (1, 8)), (0, 1, 32, 2.75))
    return dict(queries=queries, keys=keys, values=values, out_weight=out_weight, out_grad=out_grad)


grad_scale = 0.015625


def pair_mean(x):
    wide = x.astype(jnp.float32).reshape((x.shape[0] // 2, 2) + x.shape[1:])
    return (0.5 * jnp.sum(wide, axis=1)).astype(jnp.bfloat16)


def spread_pairs(grad):
    return 0.5 * jnp.repeat(grad, 2, axis=0)


def swap_blocks(x):
    split = (x.shape[0] // (2 * BLOCK), 2, BLOCK) + x.shape[1:]
    return jnp.flip(x.reshape(split), 1).reshape(x.shape)


def blocked(x):
    return x.reshape((x.shape[0] // BLOCK, BLOCK) + x.shape[1:])


def key_blocks(x):
    levels = [x]
    for level in range(1, LEVELS):
        levels.append(pair_mean(levels[-1]))
    return [blocked(x)] + [blocked(swap_blocks(layer)) for layer in levels]


def grouped(x, count):
    return x.reshape((count, x.shape[0] // count) + x.shape[1:]).astype(jnp.float32)


def forward_head(query, key_rows, value_rows):
    scale = HEAD_DIM ** -0.5
    kb = key_blocks(key_rows)
    vb = key_blocks(value_rows)
    count_rows, heads = query.shape[0], query.shape[1]
    pieces = [jnp.einsum('gthe,gkhe->gthk', grouped(query, b.shape[0]), b.astype(jnp.float32)).reshape(count_rows, heads, BLOCK) for b in kb]
    scores = jnp.concatenate(pieces, axis=2) * scale
    top = jnp.max(scores, axis=2, keepdims=True)
    expo = jnp.exp(scores - top)
    prob = expo / jnp.sum(expo, axis=2, keepdims=True)
    weights = prob.astype(jnp.bfloat16)
    out = jnp.zeros(query.shape, jnp.float32)
    for index, b in enumerate(vb):
        part = weights[:, :, index * BLOCK:(index + 1) * BLOCK]
        out = out + jnp.einsum('gthk,gkhe->gthe', grouped(part, b.shape[0]), b.astype(jnp.float32)).reshape(query.shape)
    return prob, weights, out.astype(jnp.bfloat16), kb, vb


def fold_back(direct):
    total = swap_blocks(direct[LEVELS])
    for level in range(LEVELS - 2, 0, -1):
        total = swap_blocks(direct[level + 1]) + spread_pairs(total)
    return (direct[0] + swap_blocks(direct[1]) + spread_pairs(total)).astype(jnp.bfloat16)


def backward_head(query, key_rows, value_rows, grad_out):
    scale = HEAD_DIM ** -0.5
    prob, weights, unused, kb, vb = forward_head(query, key_rows, value_rows)
    count_rows, heads = query.shape[0], query.shape[1]
    dprob = jnp.concatenate([jnp.einsum('gthe,gkhe->gthk', grouped(grad_out, b.shape[0]), b.astype(jnp.float32)).reshape(count_rows, heads, BLOCK) for b in vb], axis=2)
    delta = jnp.sum(prob * dprob, axis=2, keepdims=True)
    dscore = (prob * (dprob - delta) * scale).astype(jnp.bfloat16)
    grad_query = jnp.zeros(query.shape, jnp.float32)
    key_direct = []
    value_direct = []
    for index in range(len(kb)):
        count = kb[index].shape[0]
        window = slice(index * BLOCK, (index + 1) * BLOCK)
        dsc = grouped(dscore[:, :, window], count)
        wts = grouped(weights[:, :, window], count)
        grad_query = grad_query + jnp.einsum('gthk,gkhe->gthe', dsc, kb[index].astype(jnp.float32)).reshape(query.shape)
        key_direct.append(jnp.einsum('gthk,gthe->gkhe', dsc, grouped(query, count)).reshape((count * BLOCK,) + query.shape[1:]))
        value_direct.append(jnp.einsum('gthk,gthe->gkhe', wts, grouped(grad_out, count)).reshape((count * BLOCK,) + query.shape[1:]))
    return grad_query.astype(jnp.bfloat16), fold_back(key_direct), fold_back(value_direct)


def reference(queries, keys, values, out_weight, out_grad):
    count_rows = queries.shape[0]

    def heads_first(x):
        return x.reshape(count_rows, HEADS, 1, HEAD_DIM).transpose(1, 0, 2, 3)

    def heads_last(x):
        return x.transpose(1, 0, 2, 3).reshape(count_rows, HEADS * HEAD_DIM)

    query_heads = heads_first(queries)
    key_heads = heads_first(keys)
    value_heads = heads_first(values)
    attention = heads_last(lax.map(lambda a: forward_head(a[0], a[1], a[2])[2], (query_heads, key_heads, value_heads)))
    group_width = (HEADS * HEAD_DIM) // HEAD_GROUPS
    mixed = jnp.zeros((count_rows, D), jnp.float32)
    for group in range(HEAD_GROUPS):
        columns = slice(group * group_width, (group + 1) * group_width)
        part = jnp.dot(attention[:, columns], out_weight[:, columns].T, preferred_element_type=jnp.float32)
        mixed = mixed + lax.optimization_barrier(part.astype(jnp.bfloat16)).astype(jnp.float32)
    mixed = mixed.astype(jnp.bfloat16)
    grad_attention = jnp.dot(out_grad, out_weight, preferred_element_type=jnp.float32).astype(jnp.bfloat16)
    grad_weight = jnp.dot(out_grad.T, attention, preferred_element_type=jnp.float32) * grad_scale
    grads = lax.map(lambda a: backward_head(a[0], a[1], a[2], a[3]), (query_heads, key_heads, value_heads, heads_first(grad_attention)))
    return mixed, heads_last(grads[0]), heads_last(grads[1]), heads_last(grads[2]), grad_weight
```

```python
import functools

import jax
import jax.numpy as jnp
from jax import lax
from jax.experimental import pallas as pl
from jax.experimental.pallas import tpu as pltpu
from jax.sharding import PartitionSpec as P

HEAD_DIM = 128
BLOCK = 16
WIDTH = 512
HEADS = WIDTH // HEAD_DIM
ROWS = 256
HALF = 128
LOCAL_KEYS = 240
FAR = 96
KEYS = LOCAL_KEYS + FAR
GRAD_SCALE = 0.015625
BF = jnp.bfloat16
F32 = jnp.float32
SMALL = pltpu.CompilerParams(vmem_limit_bytes=16 << 20)
LARGE = pltpu.CompilerParams(vmem_limit_bytes=60 << 20)
ANY = pl.BlockSpec(memory_space=pl.ANY)


def dot(a, b, dims=((1,), (0,))):
    return lax.dot_general(a, b, (dims, ((), ())), preferred_element_type=F32)


def grid_of(shape):
    return lax.broadcasted_iota(jnp.int32, shape, 0), lax.broadcasted_iota(jnp.int32, shape, 1)


def matrix(cond, value=1.0):
    return jnp.where(cond, value, 0.0).astype(BF)


def whole(x):
    return pl.BlockSpec(x.shape, lambda i, rank=len(x.shape): (0,) * rank)


def cost(micros):
    return pl.CostEstimate(flops=0, bytes_accessed=int(micros * 3.7e6), transcendentals=0)


def call(kernel, outs, *args, params=SMALL, micros=0.3):
    return pl.pallas_call(
        kernel,
        grid=(1,),
        out_shape=outs,
        in_specs=[whole(a) for a in args],
        out_specs=jax.tree.map(whole, outs),
        compiler_params=params,
        cost_estimate=cost(micros),
    )(*args)


def shaped(shape, dtype=BF):
    return jax.ShapeDtypeStruct(shape, dtype)


def pool_kernel(inputs, low, pack, high):
    for side in range(2):
        cols = slice(side * WIDTH, (side + 1) * WIDTH)
        layer = inputs[:, (side + 1) * WIDTH : (side + 2) * WIDTH]
        at = 0
        rows = ROWS
        while rows > BLOCK:
            i, j = grid_of((rows // 2, rows))
            layer = dot(matrix(j >> 1 == i, 0.5), layer).astype(BF)
            rows //= 2
            if rows > BLOCK:
                low[at : at + rows, cols] = layer
                at += rows
        pack[0:BLOCK, cols] = layer
        i, j = grid_of((BLOCK, BLOCK))
        halve = matrix(j >> 1 == i, 0.5)
        total = jnp.zeros((BLOCK, WIDTH), F32)
        at, rows = 0, BLOCK
        while rows > 1:
            layer = dot(halve, layer).astype(BF)
            rows //= 2
            total += dot(matrix((i - at == j) & (j < rows)), layer)
            at += rows
        top = total.astype(BF)
        pack[BLOCK : 2 * BLOCK, cols] = top
        high[:, cols] = top


def relay_kernel(own, first, x1, x2, x3, out7, out8):
    x = jnp.concatenate([own[...], first[BLOCK:, :], x1[...], x2[...], x3[...]], axis=0)
    i, j = grid_of((BLOCK, 8 * BLOCK))
    out7[...] = dot(matrix(j == (i >> 1) * BLOCK + 12 + (i & 1)), x).astype(BF)
    out8[...] = dot(matrix((j == i * BLOCK + 14) & (i < 8)), x).astype(BF)


def key_columns(inputs, low, far, half, low_cols):
    return jnp.concatenate(
        [
            inputs[half * HALF : (half + 1) * HALF, WIDTH + low_cols.start : WIDTH + low_cols.stop],
            low[half * 64 : (half + 1) * 64, low_cols],
            low[128 + half * 32 : 128 + (half + 1) * 32, low_cols],
            low[192 + (1 - half) * 16 : 192 + (2 - half) * 16, low_cols],
            far[:, low_cols],
        ],
        axis=0,
    )


def visible():
    k, t = grid_of((KEYS, HALF))
    seen = (k < 128) & (k >> 5 == t >> 5)
    seen |= (k >= 128) & (k < 192) & ((k - 128) >> 4 == (t >> 5) ^ 1)
    seen |= (k >= 192) & (k < 224) & ((k - 192) >> 4 == (t >> 6) ^ 1)
    seen |= (k >= 224) & (k < LOCAL_KEYS + 64)
    seen |= (k >= LOCAL_KEYS + 64) & (((k - LOCAL_KEYS) & 15) < 8)
    return seen


def forward_kernel(
    weight, inputs, low, r1, x1, x2, x3, s1, s2, s3, attention, prob, far, shares, held, sems
):
    copies = []
    for n in range(8):
        rows = slice(n * WIDTH, (n + 1) * WIDTH)
        copies.append(pltpu.make_async_copy(weight.at[rows, :], held.at[n], sems.at[n]))
        copies[-1].start()
    x = jnp.concatenate([x1[...], x2[...], x3[...]], axis=0)
    i, j = grid_of((2 * BLOCK, 6 * BLOCK))
    five = (i < BLOCK) & (j == (i >> 3) * BLOCK + (i & 7))
    n = i - BLOCK
    six = (i >= BLOCK) & (j == 2 * BLOCK + (n >> 2) * BLOCK + 8 + (n & 3))
    far[0:16, :] = r1[0:16, :]
    far[16:48, :] = dot(matrix(five | six), x).astype(BF)
    far[48:64, :] = s1[...]
    far[64:80, :] = s2[...]
    far[80:96, :] = s3[...]
    seen = visible()
    scale = HEAD_DIM ** (-0.5)
    for head in range(HEADS):
        cols = slice(head * HEAD_DIM, (head + 1) * HEAD_DIM)
        vcols = slice(WIDTH + head * HEAD_DIM, WIDTH + (head + 1) * HEAD_DIM)
        for half in range(2):
            rows = slice(half * HALF, (half + 1) * HALF)
            kc = key_columns(inputs, low, far, half, cols)
            vc = key_columns(inputs, low, far, half, vcols)
            scores = dot(kc, inputs[rows, cols], ((1,), (1,))) * scale
            scores = jnp.where(seen, scores, -1e30)
            expo = jnp.exp(scores - jnp.max(scores, axis=0, keepdims=True))
            p = expo / jnp.sum(expo, axis=0, keepdims=True)
            prob[head * 2 + half] = p
            attention[rows, cols] = dot(p.astype(BF), vc, ((0,), (0,))).astype(BF)
    att = attention[...]
    for n in range(8):
        copies[n].wait()
        shares[n] = dot(att, held[n], ((1,), (1,))).astype(BF)


def backward_kernel(inputs, low, far, prob, grad, grad_queries, local, direct, m7, m8a, m8b):
    scale = HEAD_DIM ** (-0.5)
    t, j = grid_of((HALF, 112))
    fold = (
        matrix((j < 64) & (t >> 1 == j), 0.5)
        + matrix((j >= 64) & (j < 96) & (t >> 2 == j - 64), 0.25)
        + matrix((j >= 96) & (t >> 3 == j - 96), 0.125)
    )
    for head in range(HEADS):
        cols = slice(head * HEAD_DIM, (head + 1) * HEAD_DIM)
        vcols = slice(WIDTH + head * HEAD_DIM, WIDTH + (head + 1) * HEAD_DIM)
        parts = []
        for half in range(2):
            rows = slice(half * HALF, (half + 1) * HALF)
            kc = key_columns(inputs, low, far, half, cols)
            vc = key_columns(inputs, low, far, half, vcols)
            g = grad[rows, cols]
            p = prob[head * 2 + half]
            dprob = dot(vc, g, ((1,), (1,)))
            delta = jnp.sum(p * dprob, axis=0, keepdims=True)
            dscore = (p * (dprob - delta) * scale).astype(BF)
            grad_queries[rows, cols] = dot(dscore, kc, ((0,), (0,))).astype(BF)
            parts.append((dot(dscore, inputs[rows, cols]), dot(p.astype(BF), g)))
        for side, out_cols in enumerate((cols, vcols)):
            a, b = parts[0][side], parts[1][side]
            for half, (mine, other) in enumerate(((a, b), (b, a))):
                coarse = jnp.concatenate([mine[128:224], other[224:240]], axis=0).astype(BF)
                local[half * HALF : (half + 1) * HALF, out_cols] = mine[0:128] + dot(fold, coarse)
            remote = (a[LOCAL_KEYS:] + b[LOCAL_KEYS:]).astype(BF)
            direct[:, out_cols] = remote[0:48]
            m7[:, out_cols] = remote[48:64]
            m8a[:, out_cols] = remote[64:80]
            m8b[:, out_cols] = remote[80:96]


def relay_back_kernel(direct, t1, t2, t3, pair, u1, u2, u3):
    x = jnp.concatenate([direct[16:48, :], t1[...], t2[...], t3[...]], axis=0)
    n, j = grid_of((8 * BLOCK, 5 * BLOCK))
    m, i = n >> 4, n & 15
    pick = (i < 8) & (m >= 2) & (m < 4) & (j == (m - 2) * 8 + i)
    pick |= (i >= 8) & (i < 12) & (m >= 4) & (j == 16 + (m - 4) * 4 + (i - 8))
    pick |= (i >= 12) & (i < 14) & (j == 32 + 2 * m + (i - 12))
    pick |= (i == 14) & ((j == 48 + m) | (j == 64 + m))
    y = dot(matrix(pick), x).astype(BF)
    pair[...] = y[0:32]
    u1[...] = y[32:64]
    u2[...] = y[64:96]
    u3[...] = y[96:128]


def pair_kernel(direct, pair, v1, v2, v3, own, mate):
    total = pair[...].astype(F32)
    for v in (v1, v2, v3):
        total += v[...].astype(F32)
    own[...] = total[0:16].astype(BF)
    mate[0:16, :] = direct[0:16, :]
    mate[16:32, :] = total[16:32].astype(BF)


def finish_kernel(local, own, came, grad_keys, grad_values):
    x = jnp.concatenate([came[...], own[...]], axis=0)
    t, j = grid_of((ROWS, 3 * BLOCK))
    i = j & 15
    high = j >= BLOCK
    spread = (
        matrix((j < BLOCK) & (t >> 4 == j), 0.5**4)
        + matrix(high & (i < 8) & (t >> 5 == i), 0.5**5)
        + matrix(high & (i >= 8) & (i < 12) & (t >> 6 == i - 8), 0.5**6)
        + matrix(high & (i >= 12) & (i < 14) & (t >> 7 == i - 12), 0.5**7)
        + matrix(high & (i == 14), 0.5**8)
    )
    for side, out in enumerate((grad_keys, grad_values)):
        cols = slice(side * WIDTH, (side + 1) * WIDTH)
        out[...] = (local[:, cols] + dot(spread, x[:, cols])).astype(BF)


def chunk_of(step):
    z = lax.axis_index("tp")
    return lax.rem(z + (8 + step), 8)


def columns_of(step):
    return pl.ds(pl.multiple_of(chunk_of(step) * WIDTH, WIDTH), WIDTH)


OFFSETS = (0, -1, 1, -2, 2, -3, 3, 4)


def product_kernel(*refs):
    blocks, attention, weight = refs[:9], refs[9], refs[10]
    near, away, grad = refs[11:14]
    att_held, held, weight_held, near_held, away_held, sems = refs[14:]
    copies = [pltpu.make_async_copy(attention, att_held, sems.at[0])]
    for k in range(7):
        copies.append(pltpu.make_async_copy(blocks[k], held.at[k], sems.at[1 + k]))
    copies.append(pltpu.make_async_copy(blocks[7], held.at[7, 0:HALF], sems.at[8]))
    copies.append(pltpu.make_async_copy(blocks[8], held.at[7, HALF:ROWS], sems.at[9]))
    for k, offset in enumerate(OFFSETS):
        copies.append(
            pltpu.make_async_copy(weight.at[columns_of(offset), :], weight_held.at[k], sems.at[10 + k])
        )
    for c in copies:
        c.start()
    rank = lax.axis_index("ctx")
    core = rank & 1
    place = rank >> 1
    copies[0].wait()
    att = att_held[...]
    for k, offset in enumerate(OFFSETS):
        copies[1 + k].wait()
        if k == 7:
            copies[9].wait()
        z = chunk_of(offset)
        for side, out in enumerate((near_held, away_held)):
            for pair in range(2):
                at = pl.multiple_of((2 * pair + (core ^ side)) * 128, 128)
                term = (dot(held[k, :, pl.ds(at, 128)], att, ((0,), (0,))) * GRAD_SCALE).astype(BF)
                apart = (2 * z + pair) ^ place
                kx, ky = apart & 3, apart >> 2
                out[0, kx * 4 + ky] = term[:, :256]
                out[1, ky * 4 + kx] = term[:, 256:]
    stores = [
        pltpu.make_async_copy(away_held, away, sems.at[18]),
        pltpu.make_async_copy(near_held, near, sems.at[19]),
    ]
    for c in stores:
        c.start()
    total = jnp.zeros((ROWS, WIDTH), F32)
    for k in range(8):
        copies[10 + k].wait()
        total += dot(held[k], weight_held[k])
    grad[...] = total.astype(BF)
    for c in stores:
        c.wait()


def ctx_exchange(x, dy=0, dx=0, dc=0):
    pairs = []
    for rank in range(32):
        y, xx, c = rank >> 3, (rank >> 1) & 3, rank & 1
        pairs.append((rank, (((y ^ dy) << 2 | (xx ^ dx)) << 1) | (c ^ dc)))
    return lax.ppermute(x, "ctx", pairs)


def shift(x, step):
    return lax.ppermute(x, "tp", [(i, (i + step) % 8) for i in range(8)])


def gather_blocks(x):
    right = left = x
    blocks = [x]
    for _ in range(3):
        right, left = shift(right, 1), shift(left, -1)
        blocks += [right, left]
    return blocks + [shift(right[:HALF], 1), shift(left[HALF:], -1)]


def total_of(*terms):
    return functools.reduce(lambda a, b: a + b, [t.astype(F32) for t in terms])


def together(*xs):
    return lax.optimization_barrier(xs)


def send_blocks(held, count, last):
    moved = [[], []]
    for k in (2, 1, 3):
        for side in range(2):
            step = {"dx" if (side == 0) != last else "dy": k}
            moved[side].append(ctx_exchange(held[side][k * count : (k + 1) * count], **step))
    return moved


def on_device(queries, keys, values, out_weight, out_grad):
    tile = shaped((ROWS, WIDTH))
    half = shaped((HALF, WIDTH))
    pack16, pack32 = shaped((16, 2 * WIDTH)), shaped((32, 2 * WIDTH))

    r1, l1 = shift(out_grad, 1), shift(out_grad, -1)
    inputs = jnp.concatenate([queries, keys, values], axis=1)
    low, pack, high = call(
        pool_kernel, (shaped((224, 2 * WIDTH)), pack32, pack16), inputs, micros=2
    )
    first = ctx_exchange(pack, dc=1)

    both = jnp.concatenate([high, first[BLOCK:]], axis=0)
    r1, l1, both = together(r1, l1, both)
    r2, l2 = shift(r1, 1), shift(l1, -1)
    row = [ctx_exchange(both, dx=k) for k in (1, 2, 3)]

    out7, out8 = call(relay_kernel, (pack16,) * 2, high, first, *row)
    r2, l2, out7, out8 = together(r2, l2, out7, out8)
    r3, l3 = shift(r2, 1), shift(l2, -1)
    column = [ctx_exchange(out7, dy=1), ctx_exchange(out8, dy=2), ctx_exchange(out8, dy=3)]

    r3, l3, *column = together(r3, l3, *column)
    r4, l4 = shift(r3[:HALF], 1), shift(l3[HALF:], -1)
    operands = (inputs, low, first, *row, *column)
    outs = (tile, shaped((2 * HEADS, KEYS, HALF), F32), shaped((FAR, 2 * WIDTH)), shaped((8, ROWS, WIDTH)))
    attention, prob, far, shares = pl.pallas_call(
        forward_kernel,
        grid=(1,),
        out_shape=outs,
        in_specs=[ANY] + [whole(x) for x in operands],
        out_specs=tuple(whole(x) for x in outs),
        scratch_shapes=[pltpu.VMEM((8, WIDTH, WIDTH), BF), pltpu.SemaphoreType.DMA((8,))],
        compiler_params=LARGE,
        cost_estimate=cost(0),
    )(out_weight, *operands)
    mixed = lax.psum_scatter(shares.reshape(8 * ROWS, WIDTH), "tp", scatter_dimension=0, tiled=True)

    blocks = [out_grad, r1, l1, r2, l2, r3, l3, r4, l4]
    parts = shaped((2, 16, 128, 256))
    near, away, grad_attention = pl.pallas_call(
        product_kernel,
        grid=(1,),
        out_shape=(parts, parts, tile),
        in_specs=[ANY] * 11,
        out_specs=(ANY, ANY, whole(tile)),
        scratch_shapes=[
            pltpu.VMEM((ROWS, WIDTH), BF),
            pltpu.VMEM((8, ROWS, WIDTH), BF),
            pltpu.VMEM((8, WIDTH, WIDTH), BF),
            pltpu.VMEM((2, 16, 128, 256), BF),
            pltpu.VMEM((2, 16, 128, 256), BF),
            pltpu.SemaphoreType.DMA((20,)),
        ],
        compiler_params=LARGE,
        cost_estimate=cost(0),
    )(*blocks, attention, out_weight)

    back = ctx_exchange(away, dc=1)
    grad_queries, local, direct, m7, m8a, m8b = call(
        backward_kernel,
        (tile, shaped((ROWS, 2 * WIDTH), F32), shaped((48, 2 * WIDTH))) + (pack16,) * 3,
        inputs, low, far, prob, grad_attention, params=LARGE, micros=0,
    )

    held = [total_of(near[side], back[side]).astype(BF) for side in range(2)]
    direct, m7, m8a, m8b, *held = together(direct, m7, m8a, m8b, *held)
    moved = send_blocks(held, 4, False)
    column = [ctx_exchange(m7, dy=1), ctx_exchange(m8a, dy=2), ctx_exchange(m8b, dy=3)]

    held = [total_of(held[side][:4], *moved[side]).astype(BF) for side in range(2)]
    moved = send_blocks(held, 1, True)
    pair, *sent = call(relay_back_kernel, (pack32,) * 4, direct, *column)
    came = [ctx_exchange(sent[k - 1], dx=k) for k in (1, 2, 3)]

    own, mate = call(pair_kernel, (pack16, pack32), direct, pair, *came)
    came = ctx_exchange(mate, dc=1)
    held = [total_of(held[side][:1], *moved[side]) for side in range(2)]
    grad_weight = jnp.concatenate([h[0] for h in held], axis=1)

    grad_keys, grad_values = call(finish_kernel, (tile,) * 2, local, own, came)
    return mixed, grad_queries, grad_keys, grad_values, grad_weight


def solution(mesh):
    in_specs = (P("ctx", "tp"), P("ctx", "tp"), P("ctx", "tp"), P(None, "tp"), P("ctx", "tp"))
    out_specs = (P("ctx", "tp"),) * 5
    return jax.shard_map(
        on_device, mesh=mesh, in_specs=in_specs, out_specs=out_specs, check_vma=False
    )
```

```python
import jax
import jax.numpy as jnp
from jax import lax
from jax.experimental import pallas as pl
from jax.experimental.pallas import tpu as pltpu
from jax.sharding import PartitionSpec as P

HEAD_DIM = 128
BLOCK = 16
WIDTH = 512
HEADS = WIDTH // HEAD_DIM
ROWS = 256
HALF = 128
LOCAL_KEYS = 240
FAR = 96
KEYS = LOCAL_KEYS + FAR
GRAD_SCALE = 0.015625
BF = jnp.bfloat16
F32 = jnp.float32
SMALL = pltpu.CompilerParams(vmem_limit_bytes=16 << 20)
LARGE = pltpu.CompilerParams(vmem_limit_bytes=60 << 20)
ANY = pl.BlockSpec(memory_space=pl.ANY)


def dot(a, b, dims=((1,), (0,))):
    return lax.dot_general(a, b, (dims, ((), ())), preferred_element_type=F32)


def grid_of(shape):
    return lax.broadcasted_iota(jnp.int32, shape, 0), lax.broadcasted_iota(jnp.int32, shape, 1)


def matrix(cond, value=1.0):
    return jnp.where(cond, value, 0.0).astype(BF)


def whole(x):
    return pl.BlockSpec(x.shape, lambda i, rank=len(x.shape): (0,) * rank)


def cost(micros):
    return pl.CostEstimate(flops=0, bytes_accessed=int(micros * 3.7e6), transcendentals=0)


def call(kernel, outs, *args, params=SMALL, micros=0.3):
    return pl.pallas_call(
        kernel,
        grid=(1,),
        out_shape=outs,
        in_specs=[whole(a) for a in args],
        out_specs=jax.tree.map(whole, outs),
        compiler_params=params,
        cost_estimate=cost(micros),
    )(*args)


def shaped(shape, dtype=BF):
    return jax.ShapeDtypeStruct(shape, dtype)


def pool_kernel(keys, values, low, pack, high):
    for side, src in enumerate((keys, values)):
        cols = slice(side * WIDTH, (side + 1) * WIDTH)
        layer = src[...]
        at = 0
        rows = ROWS
        while rows > BLOCK:
            i, j = grid_of((rows // 2, rows))
            layer = dot(matrix(j >> 1 == i, 0.5), layer).astype(BF)
            rows //= 2
            if rows > BLOCK:
                low[at : at + rows, cols] = layer
                at += rows
        pack[0:BLOCK, cols] = layer
        i, j = grid_of((BLOCK, BLOCK))
        halve = matrix(j >> 1 == i, 0.5)
        total = jnp.zeros((BLOCK, WIDTH), F32)
        at, rows = 0, BLOCK
        while rows > 1:
            layer = dot(halve, layer).astype(BF)
            rows //= 2
            total += dot(matrix((i - at == j) & (j < rows)), layer)
            at += rows
        top = total.astype(BF)
        pack[BLOCK : 2 * BLOCK, cols] = top
        high[:, cols] = top


def relay_kernel(own, first, x1, x2, x3, out7, out8):
    x = jnp.concatenate([own[...], first[BLOCK:, :], x1[...], x2[...], x3[...]], axis=0)
    i, j = grid_of((BLOCK, 8 * BLOCK))
    out7[...] = dot(matrix(j == (i >> 1) * BLOCK + 12 + (i & 1)), x).astype(BF)
    out8[...] = dot(matrix((j == i * BLOCK + 14) & (i < 8)), x).astype(BF)


def key_columns(own, low, far, half, cols, low_cols):
    return jnp.concatenate(
        [
            own[half * HALF : (half + 1) * HALF, cols],
            low[half * 64 : (half + 1) * 64, low_cols],
            low[128 + half * 32 : 128 + (half + 1) * 32, low_cols],
            low[192 + (1 - half) * 16 : 192 + (2 - half) * 16, low_cols],
            far[:, low_cols],
        ],
        axis=0,
    )


def visible():
    k, t = grid_of((KEYS, HALF))
    seen = (k < 128) & (k >> 5 == t >> 5)
    seen |= (k >= 128) & (k < 192) & ((k - 128) >> 4 == (t >> 5) ^ 1)
    seen |= (k >= 192) & (k < 224) & ((k - 192) >> 4 == (t >> 6) ^ 1)
    seen |= (k >= 224) & (k < LOCAL_KEYS + 64)
    seen |= (k >= LOCAL_KEYS + 64) & (((k - LOCAL_KEYS) & 15) < 8)
    return seen


def forward_kernel(
    weight, queries, keys, values, low, r1, x1, x2, x3, s1, s2, s3,
    attention, prob_out, far, shares_out, held, prob, shares, sems
):
    copies = []
    for n in range(8):
        rows = slice(n * WIDTH, (n + 1) * WIDTH)
        copies.append(pltpu.make_async_copy(weight.at[rows, :], held.at[n], sems.at[n]))
        copies[-1].start()
    x = jnp.concatenate([x1[...], x2[...], x3[...]], axis=0)
    i, j = grid_of((2 * BLOCK, 6 * BLOCK))
    five = (i < BLOCK) & (j == (i >> 3) * BLOCK + (i & 7))
    n = i - BLOCK
    six = (i >= BLOCK) & (j == 2 * BLOCK + (n >> 2) * BLOCK + 8 + (n & 3))
    far[0:16, :] = r1[0:16, :]
    far[16:48, :] = dot(matrix(five | six), x).astype(BF)
    far[48:64, :] = s1[...]
    far[64:80, :] = s2[...]
    far[80:96, :] = s3[...]
    seen = visible()
    scale = HEAD_DIM ** (-0.5)
    for head in range(HEADS):
        cols = slice(head * HEAD_DIM, (head + 1) * HEAD_DIM)
        vcols = slice(WIDTH + head * HEAD_DIM, WIDTH + (head + 1) * HEAD_DIM)
        for half in range(2):
            rows = slice(half * HALF, (half + 1) * HALF)
            kc = key_columns(keys, low, far, half, cols, cols)
            vc = key_columns(values, low, far, half, cols, vcols)
            scores = dot(kc, queries[rows, cols], ((1,), (1,))) * scale
            scores = jnp.where(seen, scores, -1e30)
            expo = jnp.exp(scores - jnp.max(scores, axis=0, keepdims=True))
            p = expo / jnp.sum(expo, axis=0, keepdims=True)
            prob[head * 2 + half] = p
            attention[rows, cols] = dot(p.astype(BF), vc, ((0,), (0,))).astype(BF)
    stores = [pltpu.make_async_copy(prob, prob_out, sems.at[8])]
    stores[0].start()
    att = attention[...]
    for n in range(8):
        copies[n].wait()
        shares[n] = dot(att, held[n], ((1,), (1,))).astype(BF)
        stores.append(pltpu.make_async_copy(shares.at[n], shares_out.at[n], sems.at[9 + n]))
        stores[-1].start()
    for c in stores:
        c.wait()


REMOTE_COLUMNS = [side * WIDTH + head * HEAD_DIM for head in range(HEADS) for side in range(2)]


def backward_kernel(queries, keys, values, low, far, prob, grad, grad_queries, local, fine, top, first):
    scale = HEAD_DIM ** (-0.5)
    t, j = grid_of((HALF, 112))
    fold = (
        matrix((j < 64) & (t >> 1 == j), 0.5)
        + matrix((j >= 64) & (j < 96) & (t >> 2 == j - 64), 0.25)
        + matrix((j >= 96) & (t >> 3 == j - 96), 0.125)
    )
    remotes = []
    for head in range(HEADS):
        cols = slice(head * HEAD_DIM, (head + 1) * HEAD_DIM)
        vcols = slice(WIDTH + head * HEAD_DIM, WIDTH + (head + 1) * HEAD_DIM)
        parts = []
        for half in range(2):
            rows = slice(half * HALF, (half + 1) * HALF)
            kc = key_columns(keys, low, far, half, cols, cols)
            vc = key_columns(values, low, far, half, cols, vcols)
            g = grad[rows, cols]
            p = prob[head * 2 + half]
            dprob = dot(vc, g, ((1,), (1,)))
            delta = jnp.sum(p * dprob, axis=0, keepdims=True)
            dscore = (p * (dprob - delta) * scale).astype(BF)
            grad_queries[rows, cols] = dot(dscore, kc, ((0,), (0,))).astype(BF)
            parts.append((dot(dscore, queries[rows, cols]), dot(p.astype(BF), g)))
        for side, out_cols in enumerate((cols, vcols)):
            a, b = parts[0][side], parts[1][side]
            for half, (mine, other) in enumerate(((a, b), (b, a))):
                coarse = jnp.concatenate([mine[128:224], other[224:240]], axis=0).astype(BF)
                local[half * HALF : (half + 1) * HALF, out_cols] = mine[0:128] + dot(fold, coarse)
            remote = (a[LOCAL_KEYS:] + b[LOCAL_KEYS:]).astype(BF)
            remotes.append(remote)
            top[:, out_cols] = remote[0:16]
            fine[:, out_cols] = remote[16:48]
    core = lax.axis_index("ctx") & 1
    n, j = grid_of((4 * 32, FAR))
    k, i = n >> 5, n & 31
    along_y = (k > 0) & (i < 16) & (j == 32 + 16 * k + i)
    dc = (i >= 12).astype(jnp.int32)
    r = i - 12 * dc
    along_x = (i < 24) & (r < 8) & (k == 1) & (j == 16 + dc * 8 + r)
    along_x |= (i < 24) & (r >= 8) & (k >= 2) & (j == 32 + (2 * k - 4 + dc) * 4 + r - 8)
    along_x |= (i >= 24) & (i < 28) & (j == 48 + 4 * k + i - 24)
    along_x |= (i >= 28) & (i < 30) & (j == 64 + 2 * k + i - 28)
    along_x |= (i >= 30) & (j == 80 + 2 * k + i - 30)
    pick = matrix(((core == 0) & along_y) | ((core == 1) & along_x))
    for at, remote in zip(REMOTE_COLUMNS, remotes):
        got = dot(pick, remote).astype(BF)
        for n in range(4):
            row = n * 128 + at // 256 * 32
            first[row : row + 32, at % 256 : at % 256 + HEAD_DIM] = got[32 * n : 32 * (n + 1)]


def combine_kernel(near, back, coarse, keep, kept, a1, a2, a3):
    for k, out in enumerate((keep, a1, a2, a3)):
        for n in range(8):
            total = near[8 * k + n].astype(F32) + back[8 * k + n].astype(F32)
            out[n * 128 : (n + 1) * 128, :] = total.astype(BF)
    kept[...] = coarse[0:128, :]
    for k, out in ((1, a1), (2, a2), (3, a3)):
        out[1024:1152, :] = coarse[128 * k : 128 * (k + 1), :]


def sum_rows(refs, rows):
    total = refs[0][rows, :].astype(F32)
    for r in refs[1:]:
        total += r[rows, :].astype(F32)
    return total


def middle_kernel(fine, kept, keep, a1, a2, a3, keep2, kept2, u1, u2, u3):
    for k, out in enumerate((keep2, u1, u2, u3)):
        out[0:256, :] = sum_rows((keep, a1, a2, a3), slice(k * 256, (k + 1) * 256)).astype(BF)
    core = lax.axis_index("ctx") & 1
    n, j = grid_of((4 * 32, 32 + 4 * 32))
    k, i = n >> 5, n & 31
    dc, r = i >> 4, i & 15
    m = 2 * k + dc
    along_x = (r < 8) & (k == 1) & (j == dc * 8 + r)
    along_x |= (r >= 8) & (r < 12) & (k >= 2) & (j == 16 + (m - 4) * 4 + r - 8)
    along_x |= (r >= 12) & (r < 14) & (j == 64 + 2 * m + r - 12)
    along_x |= (r == 14) & ((j == 96 + m) | (j == 128 + m))
    row = j & 31
    along_y = (k == 0) & (r < 12) & (row == dc * 12 + r)
    along_y |= (k == 1) & (i < 4) & (row == 24 + i)
    along_y |= (k == 2) & (i < 2) & (row == 28 + i)
    along_y |= (k == 3) & (i < 2) & (row == 30 + i)
    pick = matrix(((core == 0) & along_x) | ((core == 1) & along_y & (j >= 32)))
    for c in range(4):
        got = [kept[32 * c : 32 * (c + 1), :]]
        got += [a[1024 + 32 * c : 1056 + 32 * c, :] for a in (a1, a2, a3)]
        y = dot(pick, jnp.concatenate([fine[:, 256 * c : 256 * (c + 1)]] + got, axis=0)).astype(BF)
        kept2[32 * c : 32 * (c + 1), :] = y[0:32]
        for k, u in ((1, u1), (2, u2), (3, u3)):
            u[256 + 32 * c : 288 + 32 * c, :] = y[32 * k : 32 * (k + 1)]


def last_kernel(top, kept, keep, u1, u2, u3, mine, own, mate):
    mine[...] = sum_rows((keep, u1, u2, u3), slice(0, 128))
    mate[0:128, :] = sum_rows((keep, u1, u2, u3), slice(128, 256)).astype(BF)
    core = lax.axis_index("ctx") & 1
    i, j = grid_of((32, 4 * 32))
    dc, r = i >> 4, i & 15
    placed = (j < 32) & (j == i)
    placed |= (r >= 12) & (r < 14) & (j == 32 + dc * 2 + r - 12)
    placed |= (r == 14) & ((j == 64 + dc) | (j == 96 + dc))
    pick = matrix(((core == 0) & (j & 31 == i)) | ((core == 1) & placed))
    for c in range(4):
        got = [kept[32 * c : 32 * (c + 1), :]]
        got += [u[256 + 32 * c : 288 + 32 * c, :] for u in (u1, u2, u3)]
        y = dot(pick, jnp.concatenate(got, axis=0)).astype(BF)
        own[:, 256 * c : 256 * (c + 1)] = y[0:16]
        mate[128 + 32 * c : 144 + 32 * c, :] = top[:, 256 * c : 256 * (c + 1)]
        mate[144 + 32 * c : 160 + 32 * c, :] = y[16:32]


def finish_kernel(local, own, mine, came, grad_keys, grad_values, grad_weight):
    core = lax.axis_index("ctx") & 1
    grad_weight[:, pl.ds(pl.multiple_of(core * 256, 256), 256)] = mine[...]
    grad_weight[:, pl.ds(pl.multiple_of(256 - core * 256, 256), 256)] = came[0:128, :].astype(F32)
    got = [came[128 + 32 * c : 160 + 32 * c, :] for c in range(4)]
    x = jnp.concatenate([jnp.concatenate(got, axis=1), own[...]], axis=0)
    t, j = grid_of((ROWS, 3 * BLOCK))
    i = j & 15
    high = j >= BLOCK
    spread = (
        matrix((j < BLOCK) & (t >> 4 == j), 0.5**4)
        + matrix(high & (i < 8) & (t >> 5 == i), 0.5**5)
        + matrix(high & (i >= 8) & (i < 12) & (t >> 6 == i - 8), 0.5**6)
        + matrix(high & (i >= 12) & (i < 14) & (t >> 7 == i - 12), 0.5**7)
        + matrix(high & (i == 14), 0.5**8)
    )
    for side, out in enumerate((grad_keys, grad_values)):
        cols = slice(side * WIDTH, (side + 1) * WIDTH)
        out[...] = (local[:, cols] + dot(spread, x[:, cols])).astype(BF)


def chunk_of(step):
    z = lax.axis_index("tp")
    return lax.rem(z + (8 + step), 8)


def columns_of(step):
    return pl.ds(pl.multiple_of(chunk_of(step) * WIDTH, WIDTH), WIDTH)


OFFSETS = (0, -1, 1, -2, 2, -3, 3, 4)


def product_kernel(*refs):
    blocks, attention, weight = refs[:9], refs[9], refs[10]
    near, away, grad = refs[11:14]
    att_held, held, weight_held, near_held, away_held, sems = refs[14:]
    copies = [pltpu.make_async_copy(attention, att_held, sems.at[0])]
    for k in range(7):
        copies.append(pltpu.make_async_copy(blocks[k], held.at[k], sems.at[1 + k]))
    copies.append(pltpu.make_async_copy(blocks[7], held.at[7, 0:HALF], sems.at[8]))
    copies.append(pltpu.make_async_copy(blocks[8], held.at[7, HALF:ROWS], sems.at[9]))
    for k, offset in enumerate(OFFSETS):
        copies.append(
            pltpu.make_async_copy(weight.at[columns_of(offset), :], weight_held.at[k], sems.at[10 + k])
        )
    for c in copies:
        c.start()
    rank = lax.axis_index("ctx")
    core = rank & 1
    place = rank >> 1
    copies[0].wait()
    sides = []
    for holder, out in ((core, near_held), (1 - core, away_held)):
        at = pl.multiple_of(holder * 256, 256)
        sides.append((holder, att_held[:, pl.ds(at, 256)], out))
    for k, offset in enumerate(OFFSETS):
        copies[1 + k].wait()
        if k == 7:
            copies[9].wait()
        z = chunk_of(offset)
        for i in range(4):
            block = held[k, :, i * 128 : (i + 1) * 128]
            apart = (2 * z + (i >> 1)) ^ place
            kx, ky = apart & 3, apart >> 2
            for holder, att, out in sides:
                slot = jnp.where(holder == 0, ky * 4 + kx, kx * 4 + ky) * 2 + ((i & 1) ^ holder)
                out[slot] = (dot(block, att, ((0,), (0,))) * GRAD_SCALE).astype(BF)
    stores = [
        pltpu.make_async_copy(away_held, away, sems.at[18]),
        pltpu.make_async_copy(near_held, near, sems.at[19]),
    ]
    for c in stores:
        c.start()
    total = jnp.zeros((ROWS, WIDTH), F32)
    for k in range(8):
        copies[10 + k].wait()
        total += dot(held[k], weight_held[k])
    grad[...] = total.astype(BF)
    for c in stores:
        c.wait()


def ctx_exchange(x, dy=0, dx=0, dc=0):
    pairs = []
    for rank in range(32):
        y, xx, c = rank >> 3, (rank >> 1) & 3, rank & 1
        pairs.append((rank, (((y ^ dy) << 2 | (xx ^ dx)) << 1) | (c ^ dc)))
    return lax.ppermute(x, "ctx", pairs)


def crossing(x, k, step):
    pairs = []
    for rank in range(32):
        y, xx, c = rank >> 3, (rank >> 1) & 3, rank & 1
        if c == step:
            y ^= k
        else:
            xx ^= k
        pairs.append((rank, (y << 2 | xx) << 1 | c))
    return lax.ppermute(x, "ctx", pairs)


def shift(x, step):
    return lax.ppermute(x, "tp", [(i, (i + step) % 8) for i in range(8)])


def gather_blocks(x):
    right = left = x
    blocks = [x]
    for _ in range(3):
        right, left = shift(right, 1), shift(left, -1)
        blocks += [right, left]
    return blocks + [shift(right[:HALF], 1), shift(left[HALF:], -1)]


def together(*xs):
    return lax.optimization_barrier(xs)


def on_device(queries, keys, values, out_weight, out_grad):
    tile = shaped((ROWS, WIDTH))
    pack16, pack32 = shaped((16, 2 * WIDTH)), shaped((32, 2 * WIDTH))

    r1, l1 = shift(out_grad, 1), shift(out_grad, -1)
    low, pack, high = call(
        pool_kernel, (shaped((224, 2 * WIDTH)), pack32, pack16), keys, values, micros=2
    )
    first = ctx_exchange(pack, dc=1)

    both = jnp.concatenate([high, first[BLOCK:]], axis=0)
    r1, l1, both = together(r1, l1, both)
    r2, l2 = shift(r1, 1), shift(l1, -1)
    row = [ctx_exchange(both, dx=k) for k in (1, 2, 3)]

    out7, out8 = call(relay_kernel, (pack16,) * 2, high, first, *row)
    r2, l2, out7, out8 = together(r2, l2, out7, out8)
    r3, l3 = shift(r2, 1), shift(l2, -1)
    column = [ctx_exchange(out7, dy=1), ctx_exchange(out8, dy=2), ctx_exchange(out8, dy=3)]

    r3, l3, *column = together(r3, l3, *column)
    r4, l4 = shift(r3[:HALF], 1), shift(l3[HALF:], -1)
    operands = (queries, keys, values, low, first, *row, *column)
    outs = (tile, shaped((2 * HEADS, KEYS, HALF), F32), shaped((FAR, 2 * WIDTH)), shaped((8, ROWS, WIDTH)))
    attention, prob, far, shares = pl.pallas_call(
        forward_kernel,
        grid=(1,),
        out_shape=outs,
        in_specs=[ANY] + [whole(x) for x in operands],
        out_specs=(whole(outs[0]), ANY, whole(outs[2]), ANY),
        scratch_shapes=[
            pltpu.VMEM((8, WIDTH, WIDTH), BF),
            pltpu.VMEM(outs[1].shape, F32),
            pltpu.VMEM(outs[3].shape, BF),
            pltpu.SemaphoreType.DMA((17,)),
        ],
        compiler_params=LARGE,
        cost_estimate=cost(8),
    )(out_weight, *operands)
    shares, r4, l4 = together(shares, r4, l4)
    mixed = lax.psum_scatter(shares.reshape(8 * ROWS, WIDTH), "tp", scatter_dimension=0, tiled=True)

    blocks = [out_grad, r1, l1, r2, l2, r3, l3, r4, l4]
    parts = shaped((32, 128, 256))
    near, away, grad_attention = pl.pallas_call(
        product_kernel,
        grid=(1,),
        out_shape=(parts, parts, tile),
        in_specs=[ANY] * 11,
        out_specs=(ANY, ANY, whole(tile)),
        scratch_shapes=[
            pltpu.VMEM((ROWS, WIDTH), BF),
            pltpu.VMEM((8, ROWS, WIDTH), BF),
            pltpu.VMEM((8, WIDTH, WIDTH), BF),
            pltpu.VMEM((32, 128, 256), BF),
            pltpu.VMEM((32, 128, 256), BF),
            pltpu.SemaphoreType.DMA((20,)),
        ],
        compiler_params=LARGE,
        cost_estimate=cost(0),
    )(*blocks, attention, out_weight)

    back = ctx_exchange(away, dc=1)
    grad_queries, local, fine, top, coarse = call(
        backward_kernel,
        (
            tile,
            shaped((ROWS, 2 * WIDTH), F32),
            shaped((32, 2 * WIDTH)),
            pack16,
            shaped((512, 256)),
        ),
        queries, keys, values, low, far, prob, grad_attention, params=LARGE, micros=0,
    )

    small, joint = shaped((128, 256)), shaped((1152, 256))
    keep, kept, *sent = call(
        combine_kernel, (shaped((1024, 256)), small) + (joint,) * 3, near, back, coarse
    )
    over = [crossing(sent[k - 1], k, 0) for k in (1, 2, 3)]
    joint = shaped((384, 256))
    keep, kept, *sent = call(
        middle_kernel, (shaped((256, 256)), small) + (joint,) * 3, fine, kept, keep, *over
    )
    over = [crossing(sent[k - 1], k, 1) for k in (1, 2, 3)]
    mixed, *over = together(mixed, *over)
    mine, own, mate = call(
        last_kernel, (shaped((128, 256), F32), pack16, shaped((256, 256))), top, kept, keep, *over
    )
    grad_keys, grad_values, grad_weight = call(
        finish_kernel, (tile, tile, shaped((128, WIDTH), F32)), local, own, mine, ctx_exchange(mate, dc=1)
    )
    return mixed, grad_queries, grad_keys, grad_values, grad_weight


def solution(mesh):
    in_specs = (P("ctx", "tp"), P("ctx", "tp"), P("ctx", "tp"), P(None, "tp"), P("ctx", "tp"))
    out_specs = (P("ctx", "tp"),) * 5
    return jax.shard_map(
        on_device, mesh=mesh, in_specs=in_specs, out_specs=out_specs, check_vma=False
    )
```

```python
import jax
import jax.numpy as jnp
from jax import lax
from jax.experimental import pallas as pl
from jax.experimental.pallas import tpu as pltpu
from jax.sharding import PartitionSpec as P

HEAD_DIM = 128
BLOCK = 16
WIDTH = 512
HEADS = WIDTH // HEAD_DIM
ROWS = 256
HALF = 128
LOCAL_KEYS = 240
FAR = 96
KEYS = LOCAL_KEYS + FAR
GRAD_SCALE = 0.015625
BF = jnp.bfloat16
F32 = jnp.float32
SMALL = pltpu.CompilerParams(vmem_limit_bytes=16 << 20)
LARGE = pltpu.CompilerParams(vmem_limit_bytes=60 << 20)
ANY = pl.BlockSpec(memory_space=pl.ANY)


def dot(a, b, dims=((1,), (0,))):
    return lax.dot_general(a, b, (dims, ((), ())), preferred_element_type=F32)


def grid_of(shape):
    return lax.broadcasted_iota(jnp.int32, shape, 0), lax.broadcasted_iota(jnp.int32, shape, 1)


def matrix(cond, value=1.0):
    return jnp.where(cond, value, 0.0).astype(BF)


def whole(x):
    return pl.BlockSpec(x.shape, lambda i, rank=len(x.shape): (0,) * rank)


def cost(micros):
    return pl.CostEstimate(flops=0, bytes_accessed=int(micros * 3.7e6), transcendentals=0)


def call(kernel, outs, *args, params=SMALL, micros=0.3):
    return pl.pallas_call(
        kernel,
        grid=(1,),
        out_shape=outs,
        in_specs=[whole(a) for a in args],
        out_specs=jax.tree.map(whole, outs),
        compiler_params=params,
        cost_estimate=cost(micros),
    )(*args)


def shaped(shape, dtype=BF):
    return jax.ShapeDtypeStruct(shape, dtype)


def pool_kernel(keys, values, low, pack, high):
    layer = jnp.concatenate([keys[...], values[...]], axis=1)
    at = 0
    rows = ROWS
    while rows > BLOCK:
        i, j = grid_of((rows // 2, rows))
        layer = dot(matrix(j >> 1 == i, 0.5), layer).astype(BF)
        rows //= 2
        if rows > BLOCK:
            low[at : at + rows, :] = layer
            at += rows
    pack[0:BLOCK, :] = layer
    i, j = grid_of((BLOCK, BLOCK))
    halve = matrix(j >> 1 == i, 0.5)
    total = jnp.zeros((BLOCK, 2 * WIDTH), F32)
    at, rows = 0, BLOCK
    while rows > 1:
        layer = dot(halve, layer).astype(BF)
        rows //= 2
        total += dot(matrix((i - at == j) & (j < rows)), layer)
        at += rows
    top = total.astype(BF)
    pack[BLOCK : 2 * BLOCK, :] = top
    high[...] = top


def relay_kernel(own, first, x1, x3, x2, out7, out8):
    x = jnp.concatenate([own[...], first[BLOCK:, :], x1[...], x2[...], x3[...]], axis=0)
    i, j = grid_of((BLOCK, 8 * BLOCK))
    out7[...] = dot(matrix(j == (i >> 1) * BLOCK + 12 + (i & 1)), x).astype(BF)
    out8[...] = dot(matrix((j == i * BLOCK + 14) & (i < 8)), x).astype(BF)


def key_columns(own, low, far, half, cols, low_cols):
    return jnp.concatenate(
        [
            own[half * HALF : (half + 1) * HALF, cols],
            low[half * 64 : (half + 1) * 64, low_cols],
            low[128 + half * 32 : 128 + (half + 1) * 32, low_cols],
            low[192 + (1 - half) * 16 : 192 + (2 - half) * 16, low_cols],
            far[:, low_cols],
        ],
        axis=0,
    )


def visible():
    k, t = grid_of((KEYS, HALF))
    seen = (k < 128) & (k >> 5 == t >> 5)
    seen |= (k >= 128) & (k < 192) & ((k - 128) >> 4 == (t >> 5) ^ 1)
    seen |= (k >= 192) & (k < 224) & ((k - 192) >> 4 == (t >> 6) ^ 1)
    seen |= (k >= 224) & (k < LOCAL_KEYS + 64)
    seen |= (k >= LOCAL_KEYS + 64) & (((k - LOCAL_KEYS) & 15) < 8)
    return seen


def forward_kernel(
    weight, queries, keys, values, low, r1, x1, x3, x2, s1, s3, s2,
    attention, prob_out, far, shares_out, held, prob, shares, sems
):
    copies = []
    for n in range(8):
        rows = slice(n * WIDTH, (n + 1) * WIDTH)
        copies.append(pltpu.make_async_copy(weight.at[rows, :], held.at[n], sems.at[n]))
        copies[-1].start()
    x = jnp.concatenate([x1[...], x2[...], x3[...]], axis=0)
    i, j = grid_of((2 * BLOCK, 6 * BLOCK))
    five = (i < BLOCK) & (j == (i >> 3) * BLOCK + (i & 7))
    n = i - BLOCK
    six = (i >= BLOCK) & (j == 2 * BLOCK + (n >> 2) * BLOCK + 8 + (n & 3))
    far[0:16, :] = r1[0:16, :]
    far[16:48, :] = dot(matrix(five | six), x).astype(BF)
    far[48:64, :] = s1[...]
    far[64:80, :] = s2[...]
    far[80:96, :] = s3[...]
    seen = visible()
    scale = HEAD_DIM ** (-0.5)
    for head in range(HEADS):
        cols = slice(head * HEAD_DIM, (head + 1) * HEAD_DIM)
        vcols = slice(WIDTH + head * HEAD_DIM, WIDTH + (head + 1) * HEAD_DIM)
        for half in range(2):
            rows = slice(half * HALF, (half + 1) * HALF)
            kc = key_columns(keys, low, far, half, cols, cols)
            vc = key_columns(values, low, far, half, cols, vcols)
            scores = dot(kc, queries[rows, cols], ((1,), (1,))) * scale
            scores = jnp.where(seen, scores, -1e30)
            expo = jnp.exp(scores - jnp.max(scores, axis=0, keepdims=True))
            p = expo / jnp.sum(expo, axis=0, keepdims=True)
            prob[head * 2 + half] = p
            attention[rows, cols] = dot(p.astype(BF), vc, ((0,), (0,))).astype(BF)
    stores = [pltpu.make_async_copy(prob, prob_out, sems.at[8])]
    stores[0].start()
    att = attention[...]
    for n in range(8):
        copies[n].wait()
        shares[n] = dot(att, held[n], ((1,), (1,))).astype(BF)
        stores.append(pltpu.make_async_copy(shares.at[n], shares_out.at[n], sems.at[9 + n]))
        stores[-1].start()
    for c in stores:
        c.wait()


REMOTE_COLUMNS = [side * WIDTH + head * HEAD_DIM for head in range(HEADS) for side in range(2)]


def backward_kernel(queries, keys, values, low, far, prob, grad, grad_queries, local, fine, top, first):
    scale = HEAD_DIM ** (-0.5)
    t, j = grid_of((HALF, 112))
    fold = (
        matrix((j < 64) & (t >> 1 == j), 0.5)
        + matrix((j >= 64) & (j < 96) & (t >> 2 == j - 64), 0.25)
        + matrix((j >= 96) & (t >> 3 == j - 96), 0.125)
    )
    remotes = []
    for head in range(HEADS):
        cols = slice(head * HEAD_DIM, (head + 1) * HEAD_DIM)
        vcols = slice(WIDTH + head * HEAD_DIM, WIDTH + (head + 1) * HEAD_DIM)
        parts = []
        for half in range(2):
            rows = slice(half * HALF, (half + 1) * HALF)
            kc = key_columns(keys, low, far, half, cols, cols)
            vc = key_columns(values, low, far, half, cols, vcols)
            g = grad[rows, cols]
            p = prob[head * 2 + half]
            dprob = dot(vc, g, ((1,), (1,)))
            delta = jnp.sum(p * dprob, axis=0, keepdims=True)
            dscore = (p * (dprob - delta) * scale).astype(BF)
            grad_queries[rows, cols] = dot(dscore, kc, ((0,), (0,))).astype(BF)
            parts.append((dot(dscore, queries[rows, cols]), dot(p.astype(BF), g)))
        for side, out_cols in enumerate((cols, vcols)):
            a, b = parts[0][side], parts[1][side]
            for half, (mine, other) in enumerate(((a, b), (b, a))):
                coarse = jnp.concatenate([mine[128:224], other[224:240]], axis=0).astype(BF)
                local[half * HALF : (half + 1) * HALF, out_cols] = mine[0:128] + dot(fold, coarse)
            remote = (a[LOCAL_KEYS:] + b[LOCAL_KEYS:]).astype(BF)
            remotes.append(remote)
            top[:, out_cols] = remote[0:16]
            fine[:, out_cols] = remote[16:48]
    core = lax.axis_index("ctx") & 1
    n, j = grid_of((4 * 32, FAR))
    k, i = n >> 5, n & 31
    along_y = (k > 0) & (i < 16) & (j == 32 + 16 * k + i)
    dc = (i >= 12).astype(jnp.int32)
    r = i - 12 * dc
    along_x = (i < 24) & (r < 8) & (k == 1) & (j == 16 + dc * 8 + r)
    along_x |= (i < 24) & (r >= 8) & (k >= 2) & (j == 32 + (2 * k - 4 + dc) * 4 + r - 8)
    along_x |= (i >= 24) & (i < 28) & (j == 48 + 4 * k + i - 24)
    along_x |= (i >= 28) & (i < 30) & (j == 64 + 2 * k + i - 28)
    along_x |= (i >= 30) & (j == 80 + 2 * k + i - 30)
    pick = matrix(((core == 0) & along_y) | ((core == 1) & along_x))
    for at, remote in zip(REMOTE_COLUMNS, remotes):
        got = dot(pick, remote).astype(BF)
        for n in range(4):
            row = n * 128 + at // 256 * 32
            first[row : row + 32, at % 256 : at % 256 + HEAD_DIM] = got[32 * n : 32 * (n + 1)]


def combine_kernel(near, back, coarse, keep, kept, a1, a2, a3):
    for k, out in enumerate((keep, a1, a2, a3)):
        for n in range(8):
            total = near[8 * k + n].astype(F32) + back[8 * k + n].astype(F32)
            out[n * 128 : (n + 1) * 128, :] = total.astype(BF)
    kept[...] = coarse[0:128, :]
    for k, out in ((1, a1), (2, a2), (3, a3)):
        out[1024:1152, :] = coarse[128 * k : 128 * (k + 1), :]


def sum_rows(refs, rows):
    total = refs[0][rows, :].astype(F32)
    for r in refs[1:]:
        total += r[rows, :].astype(F32)
    return total


def middle_kernel(fine, kept, keep, a2, a1, a3, keep2, kept2, u1, u2, u3):
    for k, out in enumerate((keep2, u1, u2, u3)):
        out[0:256, :] = sum_rows((keep, a1, a2, a3), slice(k * 256, (k + 1) * 256)).astype(BF)
    core = lax.axis_index("ctx") & 1
    n, j = grid_of((4 * 32, 32 + 4 * 32))
    k, i = n >> 5, n & 31
    dc, r = i >> 4, i & 15
    m = 2 * k + dc
    along_x = (r < 8) & (k == 1) & (j == dc * 8 + r)
    along_x |= (r >= 8) & (r < 12) & (k >= 2) & (j == 16 + (m - 4) * 4 + r - 8)
    along_x |= (r >= 12) & (r < 14) & (j == 64 + 2 * m + r - 12)
    along_x |= (r == 14) & ((j == 96 + m) | (j == 128 + m))
    row = j & 31
    along_y = (k == 0) & (r < 12) & (row == dc * 12 + r)
    along_y |= (k == 1) & (i < 4) & (row == 24 + i)
    along_y |= (k == 2) & (i < 2) & (row == 28 + i)
    along_y |= (k == 3) & (i < 2) & (row == 30 + i)
    pick = matrix(((core == 0) & along_x) | ((core == 1) & along_y & (j >= 32)))
    for c in range(4):
        got = [kept[32 * c : 32 * (c + 1), :]]
        got += [a[1024 + 32 * c : 1056 + 32 * c, :] for a in (a1, a2, a3)]
        y = dot(pick, jnp.concatenate([fine[:, 256 * c : 256 * (c + 1)]] + got, axis=0)).astype(BF)
        kept2[32 * c : 32 * (c + 1), :] = y[0:32]
        for k, u in ((1, u1), (2, u2), (3, u3)):
            u[256 + 32 * c : 288 + 32 * c, :] = y[32 * k : 32 * (k + 1)]


def last_kernel(top, kept, keep, u2, u1, u3, mine, own, mate):
    mine[...] = sum_rows((keep, u1, u2, u3), slice(0, 128))
    mate[0:128, :] = sum_rows((keep, u1, u2, u3), slice(128, 256)).astype(BF)
    core = lax.axis_index("ctx") & 1
    i, j = grid_of((32, 4 * 32))
    dc, r = i >> 4, i & 15
    placed = (j < 32) & (j == i)
    placed |= (r >= 12) & (r < 14) & (j == 32 + dc * 2 + r - 12)
    placed |= (r == 14) & ((j == 64 + dc) | (j == 96 + dc))
    pick = matrix(((core == 0) & (j & 31 == i)) | ((core == 1) & placed))
    for c in range(4):
        got = [kept[32 * c : 32 * (c + 1), :]]
        got += [u[256 + 32 * c : 288 + 32 * c, :] for u in (u1, u2, u3)]
        y = dot(pick, jnp.concatenate(got, axis=0)).astype(BF)
        own[:, 256 * c : 256 * (c + 1)] = y[0:16]
        mate[128 + 32 * c : 144 + 32 * c, :] = top[:, 256 * c : 256 * (c + 1)]
        mate[144 + 32 * c : 160 + 32 * c, :] = y[16:32]


def finish_kernel(local, own, mine, came, grad_keys, grad_values, grad_weight):
    core = lax.axis_index("ctx") & 1
    grad_weight[:, pl.ds(pl.multiple_of(core * 256, 256), 256)] = mine[...]
    grad_weight[:, pl.ds(pl.multiple_of(256 - core * 256, 256), 256)] = came[0:128, :].astype(F32)
    got = [came[128 + 32 * c : 160 + 32 * c, :] for c in range(4)]
    x = jnp.concatenate([jnp.concatenate(got, axis=1), own[...]], axis=0)
    t, j = grid_of((ROWS, 3 * BLOCK))
    i = j & 15
    high = j >= BLOCK
    spread = (
        matrix((j < BLOCK) & (t >> 4 == j), 0.5**4)
        + matrix(high & (i < 8) & (t >> 5 == i), 0.5**5)
        + matrix(high & (i >= 8) & (i < 12) & (t >> 6 == i - 8), 0.5**6)
        + matrix(high & (i >= 12) & (i < 14) & (t >> 7 == i - 12), 0.5**7)
        + matrix(high & (i == 14), 0.5**8)
    )
    for side, out in enumerate((grad_keys, grad_values)):
        cols = slice(side * WIDTH, (side + 1) * WIDTH)
        out[...] = (local[:, cols] + dot(spread, x[:, cols])).astype(BF)


def chunk_of(step):
    z = lax.axis_index("tp")
    return lax.rem(z + (8 + step), 8)


def columns_of(step):
    return pl.ds(pl.multiple_of(chunk_of(step) * WIDTH, WIDTH), WIDTH)


OFFSETS = (0, -1, 1, -2, 2, -3, 3, 4)


def product_kernel(*refs):
    blocks, attention, weight = refs[:9], refs[9], refs[10]
    near, away, grad = refs[11:14]
    att_held, held, weight_held, near_held, away_held, sems = refs[14:]
    copies = [pltpu.make_async_copy(attention, att_held, sems.at[0])]
    for k in range(7):
        copies.append(pltpu.make_async_copy(blocks[k], held.at[k], sems.at[1 + k]))
    copies.append(pltpu.make_async_copy(blocks[7], held.at[7, 0:HALF], sems.at[8]))
    copies.append(pltpu.make_async_copy(blocks[8], held.at[7, HALF:ROWS], sems.at[9]))
    for k, offset in enumerate(OFFSETS):
        copies.append(
            pltpu.make_async_copy(weight.at[columns_of(offset), :], weight_held.at[k], sems.at[10 + k])
        )
    for c in copies:
        c.start()
    rank = lax.axis_index("ctx")
    core = rank & 1
    place = rank >> 1
    copies[0].wait()
    sides = []
    for holder, out in ((core, near_held), (1 - core, away_held)):
        at = pl.multiple_of(holder * 256, 256)
        sides.append((holder, att_held[:, pl.ds(at, 256)], out))
    for k, offset in enumerate(OFFSETS):
        copies[1 + k].wait()
        if k == 7:
            copies[9].wait()
        z = chunk_of(offset)
        for i in range(4):
            block = held[k, :, i * 128 : (i + 1) * 128]
            apart = (2 * z + (i >> 1)) ^ place
            kx, ky = apart & 3, apart >> 2
            for holder, att, out in sides:
                slot = jnp.where(holder == 0, ky * 4 + kx, kx * 4 + ky) * 2 + ((i & 1) ^ holder)
                out[slot] = (dot(block, att, ((0,), (0,))) * GRAD_SCALE).astype(BF)
    stores = [
        pltpu.make_async_copy(away_held, away, sems.at[18]),
        pltpu.make_async_copy(near_held, near, sems.at[19]),
    ]
    for c in stores:
        c.start()
    total = jnp.zeros((ROWS, WIDTH), F32)
    for k in range(8):
        copies[10 + k].wait()
        total += dot(held[k], weight_held[k])
    grad[...] = total.astype(BF)
    for c in stores:
        c.wait()


def ctx_exchange(x, dy=0, dx=0, dc=0):
    pairs = []
    for rank in range(32):
        y, xx, c = rank >> 3, (rank >> 1) & 3, rank & 1
        pairs.append((rank, (((y ^ dy) << 2 | (xx ^ dx)) << 1) | (c ^ dc)))
    return lax.ppermute(x, "ctx", pairs)


def crossing(x, k, step):
    pairs = []
    for rank in range(32):
        y, xx, c = rank >> 3, (rank >> 1) & 3, rank & 1
        if c == step:
            y ^= k
        else:
            xx ^= k
        pairs.append((rank, (y << 2 | xx) << 1 | c))
    return lax.ppermute(x, "ctx", pairs)


def shift(x, step):
    return lax.ppermute(x, "tp", [(i, (i + step) % 8) for i in range(8)])


def gather_blocks(x):
    right = left = x
    blocks = [x]
    for _ in range(3):
        right, left = shift(right, 1), shift(left, -1)
        blocks += [right, left]
    return blocks + [shift(right[:HALF], 1), shift(left[HALF:], -1)]


def together(*xs):
    return lax.optimization_barrier(xs)


def on_device(queries, keys, values, out_weight, out_grad):
    tile = shaped((ROWS, WIDTH))
    pack16, pack32 = shaped((16, 2 * WIDTH)), shaped((32, 2 * WIDTH))

    r1, l1 = shift(out_grad, 1), shift(out_grad, -1)
    low, pack, high = call(
        pool_kernel, (shaped((224, 2 * WIDTH)), pack32, pack16), keys, values, micros=2
    )
    first = ctx_exchange(pack, dc=1)

    both = jnp.concatenate([high, first[BLOCK:]], axis=0)
    r1, l1, both = together(r1, l1, both)
    r2, l2 = shift(r1, 1), shift(l1, -1)
    row = [ctx_exchange(both, dx=k) for k in (1, 3, 2)]

    out7, out8 = call(relay_kernel, (pack16,) * 2, high, first, *row)
    r2, l2, out7, out8 = together(r2, l2, out7, out8)
    r3, l3 = shift(r2, 1), shift(l2, -1)
    column = [ctx_exchange(out7, dy=1), ctx_exchange(out8, dy=3), ctx_exchange(out8, dy=2)]

    r3, l3, *column = together(r3, l3, *column)
    r4, l4 = shift(r3[:HALF], 1), shift(l3[HALF:], -1)
    operands = (queries, keys, values, low, first, *row, *column)
    outs = (tile, shaped((2 * HEADS, KEYS, HALF), F32), shaped((FAR, 2 * WIDTH)), shaped((8, ROWS, WIDTH)))
    attention, prob, far, shares = pl.pallas_call(
        forward_kernel,
        grid=(1,),
        out_shape=outs,
        in_specs=[ANY] + [whole(x) for x in operands],
        out_specs=(whole(outs[0]), ANY, whole(outs[2]), ANY),
        scratch_shapes=[
            pltpu.VMEM((8, WIDTH, WIDTH), BF),
            pltpu.VMEM(outs[1].shape, F32),
            pltpu.VMEM(outs[3].shape, BF),
            pltpu.SemaphoreType.DMA((17,)),
        ],
        compiler_params=LARGE,
        cost_estimate=cost(8),
    )(out_weight, *operands)
    shares, r4, l4 = together(shares, r4, l4)
    mixed = lax.psum_scatter(shares.reshape(8 * ROWS, WIDTH), "tp", scatter_dimension=0, tiled=True)

    blocks = [out_grad, r1, l1, r2, l2, r3, l3, r4, l4]
    parts = shaped((32, 128, 256))
    near, away, grad_attention = pl.pallas_call(
        product_kernel,
        grid=(1,),
        out_shape=(parts, parts, tile),
        in_specs=[ANY] * 11,
        out_specs=(ANY, ANY, whole(tile)),
        scratch_shapes=[
            pltpu.VMEM((ROWS, WIDTH), BF),
            pltpu.VMEM((8, ROWS, WIDTH), BF),
            pltpu.VMEM((8, WIDTH, WIDTH), BF),
            pltpu.VMEM((32, 128, 256), BF),
            pltpu.VMEM((32, 128, 256), BF),
            pltpu.SemaphoreType.DMA((20,)),
        ],
        compiler_params=LARGE,
        cost_estimate=cost(0),
    )(*blocks, attention, out_weight)

    back = ctx_exchange(away, dc=1)
    grad_queries, local, fine, top, coarse = call(
        backward_kernel,
        (
            tile,
            shaped((ROWS, 2 * WIDTH), F32),
            shaped((32, 2 * WIDTH)),
            pack16,
            shaped((512, 256)),
        ),
        queries, keys, values, low, far, prob, grad_attention, params=LARGE, micros=0,
    )

    small, joint = shaped((128, 256)), shaped((1152, 256))
    keep, kept, *sent = call(
        combine_kernel, (shaped((1024, 256)), small) + (joint,) * 3, near, back, coarse
    )
    over = [crossing(sent[k - 1], k, 0) for k in (2, 1, 3)]
    joint = shaped((384, 256))
    keep, kept, *sent = call(
        middle_kernel, (shaped((256, 256)), small) + (joint,) * 3, fine, kept, keep, *over
    )
    over = [crossing(sent[k - 1], k, 1) for k in (2, 1, 3)]
    mixed, *over = together(mixed, *over)
    mine, own, mate = call(
        last_kernel, (shaped((128, 256), F32), pack16, shaped((256, 256))), top, kept, keep, *over
    )
    grad_keys, grad_values, grad_weight = call(
        finish_kernel, (tile, tile, shaped((128, WIDTH), F32)), local, own, mine, ctx_exchange(mate, dc=1)
    )
    return mixed, grad_queries, grad_keys, grad_values, grad_weight


def solution(mesh):
    in_specs = (P("ctx", "tp"), P("ctx", "tp"), P("ctx", "tp"), P(None, "tp"), P("ctx", "tp"))
    out_specs = (P("ctx", "tp"),) * 5
    return jax.shard_map(
        on_device, mesh=mesh, in_specs=in_specs, out_specs=out_specs, check_vma=False
    )
```

```python
import jax
import jax.numpy as jnp
from jax import lax
from jax.experimental import pallas as pl
from jax.experimental.pallas import tpu as pltpu
from jax.sharding import PartitionSpec as P

HEAD_DIM = 128
BLOCK = 16
WIDTH = 512
HEADS = WIDTH // HEAD_DIM
ROWS = 256
HALF = 128
LOCAL_KEYS = 240
FAR = 96
KEYS = LOCAL_KEYS + FAR
GRAD_SCALE = 0.015625
BF = jnp.bfloat16
F32 = jnp.float32
SMALL = pltpu.CompilerParams(vmem_limit_bytes=16 << 20)
LARGE = pltpu.CompilerParams(vmem_limit_bytes=60 << 20)
ANY = pl.BlockSpec(memory_space=pl.ANY)


def dot(a, b, dims=((1,), (0,))):
    return lax.dot_general(a, b, (dims, ((), ())), preferred_element_type=F32)


def grid_of(shape):
    return lax.broadcasted_iota(jnp.int32, shape, 0), lax.broadcasted_iota(jnp.int32, shape, 1)


def matrix(cond, value=1.0):
    return jnp.where(cond, value, 0.0).astype(BF)


def whole(x):
    return pl.BlockSpec(x.shape, lambda i, rank=len(x.shape): (0,) * rank)


def cost(micros):
    return pl.CostEstimate(flops=0, bytes_accessed=int(micros * 3.7e6), transcendentals=0)


def call(kernel, outs, *args, params=SMALL, micros=0.3):
    return pl.pallas_call(
        kernel,
        grid=(1,),
        out_shape=outs,
        in_specs=[whole(a) for a in args],
        out_specs=jax.tree.map(whole, outs),
        compiler_params=params,
        cost_estimate=cost(micros),
    )(*args)


def shaped(shape, dtype=BF):
    return jax.ShapeDtypeStruct(shape, dtype)


def pool_kernel(keys, values, low, pack, high):
    layer = jnp.concatenate([keys[...], values[...]], axis=1)
    at = 0
    rows = ROWS
    while rows > BLOCK:
        i, j = grid_of((rows // 2, rows))
        layer = dot(matrix(j >> 1 == i, 0.5), layer).astype(BF)
        rows //= 2
        if rows > BLOCK:
            low[at : at + rows, :] = layer
            at += rows
    pack[0:BLOCK, :] = layer
    i, j = grid_of((BLOCK, BLOCK))
    halve = matrix(j >> 1 == i, 0.5)
    total = jnp.zeros((BLOCK, 2 * WIDTH), F32)
    at, rows = 0, BLOCK
    while rows > 1:
        layer = dot(halve, layer).astype(BF)
        rows //= 2
        total += dot(matrix((i - at == j) & (j < rows)), layer)
        at += rows
    top = total.astype(BF)
    pack[BLOCK : 2 * BLOCK, :] = top
    high[...] = top


def relay_kernel(own, first, x1, x3, x2, out7, out8):
    x = jnp.concatenate([own[...], first[BLOCK:, :], x1[...], x2[...], x3[...]], axis=0)
    i, j = grid_of((BLOCK, 8 * BLOCK))
    out7[...] = dot(matrix(j == (i >> 1) * BLOCK + 12 + (i & 1)), x).astype(BF)
    out8[...] = dot(matrix((j == i * BLOCK + 14) & (i < 8)), x).astype(BF)


def key_columns(own, low, far, half, cols, low_cols):
    return jnp.concatenate(
        [
            own[half * HALF : (half + 1) * HALF, cols],
            low[half * 64 : (half + 1) * 64, low_cols],
            low[128 + half * 32 : 128 + (half + 1) * 32, low_cols],
            low[192 + (1 - half) * 16 : 192 + (2 - half) * 16, low_cols],
            far[:, low_cols],
        ],
        axis=0,
    )


def visible():
    k, t = grid_of((KEYS, HALF))
    seen = (k < 128) & (k >> 5 == t >> 5)
    seen |= (k >= 128) & (k < 192) & ((k - 128) >> 4 == (t >> 5) ^ 1)
    seen |= (k >= 192) & (k < 224) & ((k - 192) >> 4 == (t >> 6) ^ 1)
    seen |= (k >= 224) & (k < LOCAL_KEYS + 64)
    seen |= (k >= LOCAL_KEYS + 64) & (((k - LOCAL_KEYS) & 15) < 8)
    return seen


def forward_kernel(
    weight, queries, keys, values, low, r1, x1, x3, x2, s1, s3, s2,
    attention, prob_out, far, shares_out, held, prob, shares, sems
):
    copies = []
    for n in range(8):
        rows = slice(n * WIDTH, (n + 1) * WIDTH)
        copies.append(pltpu.make_async_copy(weight.at[rows, :], held.at[n], sems.at[n]))
        copies[-1].start()
    x = jnp.concatenate([x1[...], x2[...], x3[...]], axis=0)
    i, j = grid_of((2 * BLOCK, 6 * BLOCK))
    five = (i < BLOCK) & (j == (i >> 3) * BLOCK + (i & 7))
    n = i - BLOCK
    six = (i >= BLOCK) & (j == 2 * BLOCK + (n >> 2) * BLOCK + 8 + (n & 3))
    far[0:16, :] = r1[0:16, :]
    far[16:48, :] = dot(matrix(five | six), x).astype(BF)
    far[48:64, :] = s1[...]
    far[64:80, :] = s2[...]
    far[80:96, :] = s3[...]
    seen = visible()
    scale = HEAD_DIM ** (-0.5)
    for head in range(HEADS):
        cols = slice(head * HEAD_DIM, (head + 1) * HEAD_DIM)
        vcols = slice(WIDTH + head * HEAD_DIM, WIDTH + (head + 1) * HEAD_DIM)
        for half in range(2):
            rows = slice(half * HALF, (half + 1) * HALF)
            kc = key_columns(keys, low, far, half, cols, cols)
            vc = key_columns(values, low, far, half, cols, vcols)
            scores = dot(kc, queries[rows, cols], ((1,), (1,))) * scale
            scores = jnp.where(seen, scores, -1e30)
            expo = jnp.exp(scores - jnp.max(scores, axis=0, keepdims=True))
            p = expo / jnp.sum(expo, axis=0, keepdims=True)
            prob[head * 2 + half] = p
            attention[rows, cols] = dot(p.astype(BF), vc, ((0,), (0,))).astype(BF)
    stores = [pltpu.make_async_copy(prob, prob_out, sems.at[8])]
    stores[0].start()
    att = attention[...]
    for n in range(8):
        copies[n].wait()
        shares[n] = dot(att, held[n], ((1,), (1,))).astype(BF)
        stores.append(pltpu.make_async_copy(shares.at[n], shares_out.at[n], sems.at[9 + n]))
        stores[-1].start()
    for c in stores:
        c.wait()


REMOTE_COLUMNS = [side * WIDTH + head * HEAD_DIM for head in range(HEADS) for side in range(2)]


def backward_kernel(queries, keys, values, low, far, prob, grad, grad_queries, local, fine, top, first):
    scale = HEAD_DIM ** (-0.5)
    t, j = grid_of((HALF, 112))
    fold = (
        matrix((j < 64) & (t >> 1 == j), 0.5)
        + matrix((j >= 64) & (j < 96) & (t >> 2 == j - 64), 0.25)
        + matrix((j >= 96) & (t >> 3 == j - 96), 0.125)
    )
    remotes = []
    for head in range(HEADS):
        cols = slice(head * HEAD_DIM, (head + 1) * HEAD_DIM)
        vcols = slice(WIDTH + head * HEAD_DIM, WIDTH + (head + 1) * HEAD_DIM)
        parts = []
        for half in range(2):
            rows = slice(half * HALF, (half + 1) * HALF)
            kc = key_columns(keys, low, far, half, cols, cols)
            vc = key_columns(values, low, far, half, cols, vcols)
            g = grad[rows, cols]
            p = prob[head * 2 + half]
            dprob = dot(vc, g, ((1,), (1,)))
            delta = jnp.sum(p * dprob, axis=0, keepdims=True)
            dscore = (p * (dprob - delta) * scale).astype(BF)
            grad_queries[rows, cols] = dot(dscore, kc, ((0,), (0,))).astype(BF)
            parts.append((dot(dscore, queries[rows, cols]), dot(p.astype(BF), g)))
        for side, out_cols in enumerate((cols, vcols)):
            a, b = parts[0][side], parts[1][side]
            for half, (mine, other) in enumerate(((a, b), (b, a))):
                coarse = jnp.concatenate([mine[128:224], other[224:240]], axis=0).astype(BF)
                local[half * HALF : (half + 1) * HALF, out_cols] = mine[0:128] + dot(fold, coarse)
            remote = (a[LOCAL_KEYS:] + b[LOCAL_KEYS:]).astype(BF)
            remotes.append(remote)
            top[:, out_cols] = remote[0:16]
            fine[:, out_cols] = remote[16:48]
    core = lax.axis_index("ctx") & 1
    n, j = grid_of((4 * 32, FAR))
    k, i = n >> 5, n & 31
    along_y = (k > 0) & (i < 16) & (j == 32 + 16 * k + i)
    dc = (i >= 12).astype(jnp.int32)
    r = i - 12 * dc
    along_x = (i < 24) & (r < 8) & (k == 1) & (j == 16 + dc * 8 + r)
    along_x |= (i < 24) & (r >= 8) & (k >= 2) & (j == 32 + (2 * k - 4 + dc) * 4 + r - 8)
    along_x |= (i >= 24) & (i < 28) & (j == 48 + 4 * k + i - 24)
    along_x |= (i >= 28) & (i < 30) & (j == 64 + 2 * k + i - 28)
    along_x |= (i >= 30) & (j == 80 + 2 * k + i - 30)
    pick = matrix(((core == 0) & along_y) | ((core == 1) & along_x))
    for at, remote in zip(REMOTE_COLUMNS, remotes):
        got = dot(pick, remote).astype(BF)
        for n in range(4):
            row = n * 128 + at // 256 * 32
            first[row : row + 32, at % 256 : at % 256 + HEAD_DIM] = got[32 * n : 32 * (n + 1)]


def combine_kernel(near, back, coarse, keep, kept, a1, a2, a3, sems):
    copies = [pltpu.make_async_copy(coarse.at[0:128, :], kept, sems.at[0])]
    for k, out in ((1, a1), (2, a2), (3, a3)):
        copies.append(
            pltpu.make_async_copy(coarse.at[128 * k : 128 * (k + 1), :], out.at[1024:1152, :], sems.at[k])
        )
    for c in copies:
        c.start()
    for k, out in enumerate((keep, a1, a2, a3)):
        for n in range(8):
            total = near[8 * k + n].astype(F32) + back[8 * k + n].astype(F32)
            out[n * 128 : (n + 1) * 128, :] = total.astype(BF)
    for c in copies:
        c.wait()


def sum_rows(refs, rows):
    total = refs[0][rows, :].astype(F32)
    for r in refs[1:]:
        total += r[rows, :].astype(F32)
    return total


def middle_kernel(fine, kept, keep, a2, a1, a3, keep2, kept2, u1, u2, u3):
    for k, out in enumerate((keep2, u1, u2, u3)):
        out[0:256, :] = sum_rows((keep, a1, a2, a3), slice(k * 256, (k + 1) * 256)).astype(BF)
    core = lax.axis_index("ctx") & 1
    n, j = grid_of((4 * 32, 32 + 4 * 32))
    k, i = n >> 5, n & 31
    dc, r = i >> 4, i & 15
    m = 2 * k + dc
    along_x = (r < 8) & (k == 1) & (j == dc * 8 + r)
    along_x |= (r >= 8) & (r < 12) & (k >= 2) & (j == 16 + (m - 4) * 4 + r - 8)
    along_x |= (r >= 12) & (r < 14) & (j == 64 + 2 * m + r - 12)
    along_x |= (r == 14) & ((j == 96 + m) | (j == 128 + m))
    row = j & 31
    along_y = (k == 0) & (r < 12) & (row == dc * 12 + r)
    along_y |= (k == 1) & (i < 4) & (row == 24 + i)
    along_y |= (k == 2) & (i < 2) & (row == 28 + i)
    along_y |= (k == 3) & (i < 2) & (row == 30 + i)
    pick = matrix(((core == 0) & along_x) | ((core == 1) & along_y & (j >= 32)))
    for c in range(4):
        got = [kept[32 * c : 32 * (c + 1), :]]
        got += [a[1024 + 32 * c : 1056 + 32 * c, :] for a in (a1, a2, a3)]
        y = dot(pick, jnp.concatenate([fine[:, 256 * c : 256 * (c + 1)]] + got, axis=0)).astype(BF)
        kept2[32 * c : 32 * (c + 1), :] = y[0:32]
        for k, u in ((1, u1), (2, u2), (3, u3)):
            u[256 + 32 * c : 288 + 32 * c, :] = y[32 * k : 32 * (k + 1)]


def last_kernel(top, kept, keep, u2, u1, u3, mine, own, mate):
    mine[...] = sum_rows((keep, u1, u2, u3), slice(0, 128))
    mate[0:128, :] = sum_rows((keep, u1, u2, u3), slice(128, 256)).astype(BF)
    core = lax.axis_index("ctx") & 1
    i, j = grid_of((32, 4 * 32))
    dc, r = i >> 4, i & 15
    placed = (j < 32) & (j == i)
    placed |= (r >= 12) & (r < 14) & (j == 32 + dc * 2 + r - 12)
    placed |= (r == 14) & ((j == 64 + dc) | (j == 96 + dc))
    pick = matrix(((core == 0) & (j & 31 == i)) | ((core == 1) & placed))
    for c in range(4):
        got = [kept[32 * c : 32 * (c + 1), :]]
        got += [u[256 + 32 * c : 288 + 32 * c, :] for u in (u1, u2, u3)]
        y = dot(pick, jnp.concatenate(got, axis=0)).astype(BF)
        own[:, 256 * c : 256 * (c + 1)] = y[0:16]
        mate[128 + 32 * c : 144 + 32 * c, :] = top[:, 256 * c : 256 * (c + 1)]
        mate[144 + 32 * c : 160 + 32 * c, :] = y[16:32]


def finish_kernel(local, own, mine, came, grad_keys, grad_values, grad_weight):
    core = lax.axis_index("ctx") & 1
    grad_weight[:, pl.ds(pl.multiple_of(core * 256, 256), 256)] = mine[...]
    grad_weight[:, pl.ds(pl.multiple_of(256 - core * 256, 256), 256)] = came[0:128, :].astype(F32)
    got = [came[128 + 32 * c : 160 + 32 * c, :] for c in range(4)]
    x = jnp.concatenate([jnp.concatenate(got, axis=1), own[...]], axis=0)
    t, j = grid_of((ROWS, 3 * BLOCK))
    i = j & 15
    high = j >= BLOCK
    spread = (
        matrix((j < BLOCK) & (t >> 4 == j), 0.5**4)
        + matrix(high & (i < 8) & (t >> 5 == i), 0.5**5)
        + matrix(high & (i >= 8) & (i < 12) & (t >> 6 == i - 8), 0.5**6)
        + matrix(high & (i >= 12) & (i < 14) & (t >> 7 == i - 12), 0.5**7)
        + matrix(high & (i == 14), 0.5**8)
    )
    for side, out in enumerate((grad_keys, grad_values)):
        cols = slice(side * WIDTH, (side + 1) * WIDTH)
        out[...] = (local[:, cols] + dot(spread, x[:, cols])).astype(BF)


def chunk_of(step):
    z = lax.axis_index("tp")
    return lax.rem(z + (8 + step), 8)


def columns_of(step):
    return pl.ds(pl.multiple_of(chunk_of(step) * WIDTH, WIDTH), WIDTH)


OFFSETS = (0, -1, 1, -2, 2, -3, 3, 4)


def product_kernel(*refs):
    blocks, attention, weight = refs[:9], refs[9], refs[10]
    near, away, grad = refs[11:14]
    att_held, held, weight_held, near_held, away_held, sems = refs[14:]
    copies = [pltpu.make_async_copy(attention, att_held, sems.at[0])]
    for k in range(7):
        copies.append(pltpu.make_async_copy(blocks[k], held.at[k], sems.at[1 + k]))
    copies.append(pltpu.make_async_copy(blocks[7], held.at[7, 0:HALF], sems.at[8]))
    copies.append(pltpu.make_async_copy(blocks[8], held.at[7, HALF:ROWS], sems.at[9]))
    for k, offset in enumerate(OFFSETS):
        copies.append(
            pltpu.make_async_copy(weight.at[columns_of(offset), :], weight_held.at[k], sems.at[10 + k])
        )
    for c in copies:
        c.start()
    rank = lax.axis_index("ctx")
    core = rank & 1
    place = rank >> 1
    copies[0].wait()
    sides = []
    for holder, out in ((core, near_held), (1 - core, away_held)):
        at = pl.multiple_of(holder * 256, 256)
        sides.append((holder, att_held[:, pl.ds(at, 256)], out))
    for k, offset in enumerate(OFFSETS):
        copies[1 + k].wait()
        if k == 7:
            copies[9].wait()
        z = chunk_of(offset)
        for i in range(4):
            block = held[k, :, i * 128 : (i + 1) * 128]
            apart = (2 * z + (i >> 1)) ^ place
            kx, ky = apart & 3, apart >> 2
            for holder, att, out in sides:
                slot = jnp.where(holder == 0, ky * 4 + kx, kx * 4 + ky) * 2 + ((i & 1) ^ holder)
                out[slot] = (dot(block, att, ((0,), (0,))) * GRAD_SCALE).astype(BF)
    stores = [
        pltpu.make_async_copy(away_held, away, sems.at[18]),
        pltpu.make_async_copy(near_held, near, sems.at[19]),
    ]
    for c in stores:
        c.start()
    total = jnp.zeros((ROWS, WIDTH), F32)
    for k in range(8):
        copies[10 + k].wait()
        total += dot(held[k], weight_held[k])
    grad[...] = total.astype(BF)
    for c in stores:
        c.wait()


def ctx_exchange(x, dy=0, dx=0, dc=0):
    pairs = []
    for rank in range(32):
        y, xx, c = rank >> 3, (rank >> 1) & 3, rank & 1
        pairs.append((rank, (((y ^ dy) << 2 | (xx ^ dx)) << 1) | (c ^ dc)))
    return lax.ppermute(x, "ctx", pairs)


def crossing(x, k, step):
    pairs = []
    for rank in range(32):
        y, xx, c = rank >> 3, (rank >> 1) & 3, rank & 1
        if c == step:
            y ^= k
        else:
            xx ^= k
        pairs.append((rank, (y << 2 | xx) << 1 | c))
    return lax.ppermute(x, "ctx", pairs)


def shift(x, step):
    return lax.ppermute(x, "tp", [(i, (i + step) % 8) for i in range(8)])


def gather_blocks(x):
    right = left = x
    blocks = [x]
    for _ in range(3):
        right, left = shift(right, 1), shift(left, -1)
        blocks += [right, left]
    return blocks + [shift(right[:HALF], 1), shift(left[HALF:], -1)]


def together(*xs):
    return lax.optimization_barrier(xs)


def on_device(queries, keys, values, out_weight, out_grad):
    tile = shaped((ROWS, WIDTH))
    pack16, pack32 = shaped((16, 2 * WIDTH)), shaped((32, 2 * WIDTH))

    r1, l1 = shift(out_grad, 1), shift(out_grad, -1)
    low, pack, high = call(
        pool_kernel, (shaped((224, 2 * WIDTH)), pack32, pack16), keys, values, micros=2
    )
    first = ctx_exchange(pack, dc=1)

    both = jnp.concatenate([high, first[BLOCK:]], axis=0)
    r1, l1, both = together(r1, l1, both)
    r2, l2 = shift(r1, 1), shift(l1, -1)
    row = [ctx_exchange(both, dx=k) for k in (1, 3, 2)]

    out7, out8 = call(relay_kernel, (pack16,) * 2, high, first, *row)
    r2, l2, out7, out8 = together(r2, l2, out7, out8)
    r3, l3 = shift(r2, 1), shift(l2, -1)
    column = [ctx_exchange(out7, dy=1), ctx_exchange(out8, dy=3), ctx_exchange(out8, dy=2)]

    r3, l3, *column = together(r3, l3, *column)
    r4, l4 = shift(r3[:HALF], 1), shift(l3[HALF:], -1)
    operands = (queries, keys, values, low, first, *row, *column)
    outs = (tile, shaped((2 * HEADS, KEYS, HALF), F32), shaped((FAR, 2 * WIDTH)), shaped((8, ROWS, WIDTH)))
    attention, prob, far, shares = pl.pallas_call(
        forward_kernel,
        grid=(1,),
        out_shape=outs,
        in_specs=[ANY] + [whole(x) for x in operands],
        out_specs=(whole(outs[0]), ANY, whole(outs[2]), ANY),
        scratch_shapes=[
            pltpu.VMEM((8, WIDTH, WIDTH), BF),
            pltpu.VMEM(outs[1].shape, F32),
            pltpu.VMEM(outs[3].shape, BF),
            pltpu.SemaphoreType.DMA((17,)),
        ],
        compiler_params=LARGE,
        cost_estimate=cost(8),
    )(out_weight, *operands)
    shares, r4, l4 = together(shares, r4, l4)
    mixed = lax.psum_scatter(shares.reshape(8 * ROWS, WIDTH), "tp", scatter_dimension=0, tiled=True)

    blocks = [out_grad, r1, l1, r2, l2, r3, l3, r4, l4]
    parts = shaped((32, 128, 256))
    near, away, grad_attention = pl.pallas_call(
        product_kernel,
        grid=(1,),
        out_shape=(parts, parts, tile),
        in_specs=[ANY] * 11,
        out_specs=(ANY, ANY, whole(tile)),
        scratch_shapes=[
            pltpu.VMEM((ROWS, WIDTH), BF),
            pltpu.VMEM((8, ROWS, WIDTH), BF),
            pltpu.VMEM((8, WIDTH, WIDTH), BF),
            pltpu.VMEM((32, 128, 256), BF),
            pltpu.VMEM((32, 128, 256), BF),
            pltpu.SemaphoreType.DMA((20,)),
        ],
        compiler_params=LARGE,
        cost_estimate=cost(0),
    )(*blocks, attention, out_weight)

    back = ctx_exchange(away, dc=1)
    grad_queries, local, fine, top, coarse = call(
        backward_kernel,
        (
            tile,
            shaped((ROWS, 2 * WIDTH), F32),
            shaped((32, 2 * WIDTH)),
            pack16,
            shaped((512, 256)),
        ),
        queries, keys, values, low, far, prob, grad_attention, params=LARGE, micros=0,
    )

    small, joint = shaped((128, 256)), shaped((1152, 256))
    outs = (shaped((1024, 256)), small) + (joint,) * 3
    keep, kept, *sent = pl.pallas_call(
        combine_kernel,
        grid=(1,),
        out_shape=outs,
        in_specs=[whole(near), whole(back), ANY],
        out_specs=tuple(whole(x) for x in outs),
        scratch_shapes=[pltpu.SemaphoreType.DMA((4,))],
        compiler_params=SMALL,
        cost_estimate=cost(0.3),
    )(near, back, coarse)
    over = [crossing(sent[k - 1], k, 0) for k in (2, 1, 3)]
    joint = shaped((384, 256))
    keep, kept, *sent = call(
        middle_kernel, (shaped((256, 256)), small) + (joint,) * 3, fine, kept, keep, *over
    )
    over = [crossing(sent[k - 1], k, 1) for k in (2, 1, 3)]
    mixed, *over = together(mixed, *over)
    mine, own, mate = call(
        last_kernel, (shaped((128, 256), F32), pack16, shaped((256, 256))), top, kept, keep, *over
    )
    grad_keys, grad_values, grad_weight = call(
        finish_kernel, (tile, tile, shaped((128, WIDTH), F32)), local, own, mine, ctx_exchange(mate, dc=1)
    )
    return mixed, grad_queries, grad_keys, grad_values, grad_weight


def solution(mesh):
    in_specs = (P("ctx", "tp"), P("ctx", "tp"), P("ctx", "tp"), P(None, "tp"), P("ctx", "tp"))
    out_specs = (P("ctx", "tp"),) * 5
    return jax.shard_map(
        on_device, mesh=mesh, in_specs=in_specs, out_specs=out_specs, check_vma=False
    )
```
